128 devices in a mesh: exp: 64 (over y_lo, x, z, core), rep: 2 (over y_hi).
Axes of the slice: x: 4, y: 4 (y_hi: 2, y_lo: 2; y = y_hi * 2 + y_lo), z: 4, core: 2. Of those that a mesh axis runs over, the one named last changes fastest.
Arguments:
- tokens: bfloat16 [768, 256, 1280], P(('exp', 'rep')), may hold values from -6 to 6
- out_grad: bfloat16 [768, 256, 1280], P(('exp', 'rep')), may hold values from -12 to 12
- router: bfloat16 [64, 1280], replicated, may hold values from -1 to 1
- w_in: bfloat16 [64, 1280, 2560], P('exp'), may hold values from -0.15625 to 0.15625
- w_out: bfloat16 [64, 2560, 1280], P('exp'), may hold values from -0.125 to 0.125
Outputs:
- token_grad: bfloat16 [768, 256, 1280], P(('exp', 'rep'))
- w_in_grad: bfloat16 [64, 1280, 2560], P('exp', None, 'rep')
- w_out_grad: bfloat16 [64, 2560, 1280], P('exp', 'rep')
- router_grad: float32 [64, 1280], replicated
The draws below stay inside these ranges and needn't reach their ends.
All inputs are finite; a program needn't handle non-finite values.
Results may differ from the reference program's by a relative error of at most 0.02.
Values may be sent and summed in bfloat16 or wider, within the bound.
No kernel may reach another device: no remote copies, remote signals or barrier semaphores. Data moves between devices by JAX's collectives and lax.ppermute only.
A program may use at most 192 MiB of HBM per device.

```python
import math
import jax
import jax.numpy as jnp
from jax import lax

D = 1280
FF = 2560
TOK_IMG = 256
EXPERTS = 64
IMAGES = 768


def draw_tokens(key, part):
    key = jax.random.fold_in(key, 1)
    base_key = jax.random.fold_in(key, 0)
    values = jax.random.normal(base_key, (IMAGES, TOK_IMG, D), jnp.float32)
    return jnp.clip(values, -6.0, 6.0).astype(jnp.bfloat16)


def draw_router(key, part):
    key = jax.random.fold_in(key, 2)
    base_key = jax.random.fold_in(key, 0)
    values = jax.random.normal(base_key, (EXPERTS, D), jnp.float32) * (2.0 / math.sqrt(D))
    return jnp.clip(values, -1.0, 1.0).astype(jnp.bfloat16)


def level_of(own_key, shape, shards, low, top_value):
    gain, own = 1.0, jax.random.fold_in(own_key, 6)
    for dim, blocks in shards:
        draws = jnp.exp(jax.random.uniform(jax.random.fold_in(own, dim), (blocks,), jnp.float32, low / len(shards), top_value / len(shards)))
        gain = gain * jnp.repeat(draws, shape[dim] // blocks).reshape([-1 if axis == dim else 1 for axis in range(len(shape))])
    return gain


def gaussian(key, extent, spread, reach, cuts=(), held_as=jnp.bfloat16):
    level = level_of(key, extent, cuts, -0.22, 0.18) if cuts else 1.0
    array = jax.random.normal(key, extent, jnp.float32) * spread * level
    return jnp.minimum(jnp.maximum(array, -reach), reach).astype(held_as)


def setup_inputs(seed: int = 0) -> dict:
    keys = jax.random.split(jax.random.key(seed), 6)
    return {
        "tokens": draw_tokens(jax.random.fold_in(keys[5], 71), 0),
        "out_grad": gaussian(keys[1], (IMAGES, TOK_IMG, D), 2.0, 12.0, ((0, 128),)),
        "router": draw_router(jax.random.fold_in(keys[5], 71), 0),
        "w_in": gaussian(keys[3], (EXPERTS, D, FF), D ** -0.5, 0.15625, ((0, 64),)),
        "w_out": gaussian(keys[4], (EXPERTS, FF, D), FF ** -0.5, 0.125, ((0, 64),)),
    }


def gelu_parts(hidden):
    cdf = 0.5 * (1.0 + jax.scipy.special.erf(hidden * 0.7071067811865476))
    density = jnp.exp(-0.5 * hidden * hidden) * 0.3989422804014327
    return hidden * cdf, cdf + hidden * density


def softmax_over(logits, axis_num):
    top_val = jnp.max(logits, axis=axis_num, keepdims=True)
    expo = jnp.exp(logits - top_val)
    return expo / jnp.sum(expo, axis=axis_num, keepdims=True)


def expert_pass(item):
    row_in, row_grad, weight_in, weight_out = item
    hidden = jnp.dot(row_in, weight_in, preferred_element_type=jnp.float32)
    act_val, slope = gelu_parts(hidden)
    act = act_val.astype(jnp.bfloat16)
    row_out = jnp.dot(act, weight_out, preferred_element_type=jnp.float32).astype(jnp.bfloat16)
    dact = jnp.dot(row_grad, weight_out.T, preferred_element_type=jnp.float32)
    dhid = (dact * slope).astype(jnp.bfloat16)
    row_back = jnp.dot(dhid, weight_in.T, preferred_element_type=jnp.float32).astype(jnp.bfloat16)
    grad_in = jnp.dot(row_in.T, dhid, preferred_element_type=jnp.float32).astype(jnp.bfloat16)
    grad_out = jnp.dot(act.T, row_grad, preferred_element_type=jnp.float32).astype(jnp.bfloat16)
    return row_out, row_back, grad_in, grad_out


def reference(tokens, out_grad, router, w_in, w_out):
    tok32 = tokens.astype(jnp.float32)
    grad32 = out_grad.astype(jnp.float32)
    router32 = router.astype(jnp.float32)
    logits = jnp.einsum('sd,imd->ism', router32, tok32)
    dispatch = softmax_over(logits, 2)
    combine = softmax_over(logits, 1)
    dispatch_bf = dispatch.astype(jnp.bfloat16)
    combine_bf = combine.astype(jnp.bfloat16)
    slot_in = jnp.einsum('ism,imd->isd', dispatch_bf.astype(jnp.float32), tok32).astype(jnp.bfloat16)
    slot_grad = jnp.einsum('ism,imd->isd', combine_bf.astype(jnp.float32), grad32).astype(jnp.bfloat16)
    row_out, row_back, grad_in, grad_out = lax.map(
        expert_pass, (slot_in.transpose(1, 0, 2), slot_grad.transpose(1, 0, 2), w_in, w_out))
    slot_out = row_out.transpose(1, 0, 2).astype(jnp.float32)
    slot_back = row_back.transpose(1, 0, 2).astype(jnp.float32)
    comb_dot = jnp.einsum('imd,isd->ism', grad32, slot_out)
    disp_dot = jnp.einsum('imd,isd->ism', tok32, slot_back)
    comb_part = combine * (comb_dot - jnp.sum(combine * comb_dot, axis=1, keepdims=True))
    disp_part = dispatch * (disp_dot - jnp.sum(dispatch * disp_dot, axis=2, keepdims=True))
    logit_grad = (comb_part + disp_part).astype(jnp.bfloat16).astype(jnp.float32)
    token_grad = (jnp.einsum('ism,sd->imd', logit_grad, router32)
                  + jnp.einsum('ism,isd->imd', dispatch_bf.astype(jnp.float32), slot_back)).astype(jnp.bfloat16)
    router_grad = jnp.einsum('ism,imd->sd', logit_grad, tok32)
    return token_grad, grad_in, grad_out, router_grad
```

```python
import functools

import jax
import jax.numpy as jnp
from jax import lax
from jax.experimental import pallas as pl
from jax.experimental.pallas import tpu as pltpu
from jax.sharding import PartitionSpec as P

BF16, F32 = jnp.bfloat16, jnp.float32
NN, NT, TN = ((1,), (0,)), ((1,), (1,)), ((0,), (0,))
VMEM_LIMIT = 56 * 2**20
LANES = 128


def mm(a, b, dims):
    return lax.dot_general(a, b, (dims, ((), ())), preferred_element_type=F32)


def params():
    return pltpu.CompilerParams(vmem_limit_bytes=VMEM_LIMIT)


def gelu_parts(hidden):
    cdf = 0.5 * (1.0 + lax.erf(hidden * 0.7071067811865476))
    density = jnp.exp(-0.5 * hidden * hidden) * 0.3989422804014327
    return hidden * cdf, cdf + hidden * density


def stage_rows(packed_ref, stage_ref):
    groups, rows, _ = packed_ref.shape

    def body(g, carry):
        stage_ref[pl.ds(g, rows, stride=groups), :] = packed_ref[g].astype(F32)
        return carry

    lax.fori_loop(0, groups, body, 0, unroll=8)


def pack_rows(stage_ref, packed_ref):
    groups, rows, _ = packed_ref.shape

    def body(g, carry):
        packed_ref[g] = stage_ref[pl.ds(g, rows, stride=groups), :].astype(BF16)
        return carry

    lax.fori_loop(0, groups, body, 0, unroll=8)


def piece_rows(piece, which, first, count, images, groups):
    start = ((piece * 2 + which) * images + first) * groups
    return pl.ds(start if isinstance(start, int) else pl.multiple_of(start, groups), count * groups)


def whole_rows(stage_ref, which, first, count, images, groups):
    pieces = stage_ref.shape[0] // (2 * images * groups)
    parts = [stage_ref[piece_rows(p, which, first, count, images, groups), :] for p in range(pieces)]
    return jnp.concatenate([part.astype(BF16) for part in parts], axis=1)


def put_rows(stage_ref, value, which, first, count, images, groups):
    for p in range(value.shape[1] // LANES):
        cols = value[:, p * LANES : (p + 1) * LANES]
        stage_ref[piece_rows(p, which, first, count, images, groups), :] = cols


def gather_body(images, tokens_ref, grad_ref, router_ref, disp_ref, comb_ref, packed_ref, stage_ref):
    i = pl.program_id(0)
    slots = router_ref.shape[0]
    tok = tokens_ref[0]
    logits = mm(router_ref[...], tok, NT)
    d_exp = jnp.exp(logits - jnp.max(logits, axis=1, keepdims=True))
    dispatch = d_exp / jnp.sum(d_exp, axis=1, keepdims=True)
    c_exp = jnp.exp(logits - jnp.max(logits, axis=0, keepdims=True))
    combine = c_exp / jnp.sum(c_exp, axis=0, keepdims=True)
    disp_ref[0] = dispatch
    comb_ref[0] = combine
    slot_in = mm(dispatch.astype(BF16), tok, NN)
    slot_grad = mm(combine.astype(BF16), grad_ref[0], NN)
    put_rows(stage_ref, slot_in, 0, i, 1, images, slots)
    put_rows(stage_ref, slot_grad, 1, i, 1, images, slots)

    @pl.when(i == images - 1)
    def _():
        pack_rows(stage_ref, packed_ref)


def gather_slots(tokens, out_grad, router):
    images, toks, width = tokens.shape
    slots = router.shape[0]
    packed = (slots, 2 * images * width // LANES, LANES)
    image = lambda i: (i, 0, 0)
    return pl.pallas_call(
        functools.partial(gather_body, images),
        grid=(images,),
        in_specs=[
            pl.BlockSpec((1, toks, width), image),
            pl.BlockSpec((1, toks, width), image),
            pl.BlockSpec((slots, width), lambda i: (0, 0)),
        ],
        out_specs=[
            pl.BlockSpec((1, slots, toks), image),
            pl.BlockSpec((1, slots, toks), image),
            pl.BlockSpec(packed, lambda i: (0, 0, 0)),
        ],
        out_shape=[
            jax.ShapeDtypeStruct((images, slots, toks), F32),
            jax.ShapeDtypeStruct((images, slots, toks), F32),
            jax.ShapeDtypeStruct(packed, BF16),
        ],
        scratch_shapes=[pltpu.VMEM((packed[0] * packed[1], LANES), F32)],
        compiler_params=params(),
        name="gather_slots",
    )(tokens, out_grad, router)


def expert_body(images, packed_ref, w_in_ref, w_out_ref, act_ref, dhid_ref, back_ref,
                stage_ref, in_ref, grad_ref, out_acc, back_acc):
    f = pl.program_id(0)
    groups = packed_ref.shape[0]

    @pl.when(f == 0)
    def _():
        stage_rows(packed_ref, stage_ref)
        in_ref[...] = whole_rows(stage_ref, 0, 0, images, images, groups)
        grad_ref[...] = whole_rows(stage_ref, 1, 0, images, images, groups)

    w_in, w_out = w_in_ref[0], w_out_ref[0]
    act, slope = gelu_parts(mm(in_ref[...], w_in, NN))
    act = act.astype(BF16)
    act_ref[...] = act
    dhid = (mm(grad_ref[...], w_out, NT) * slope).astype(BF16)
    dhid_ref[...] = dhid
    row_out = mm(act, w_out, NN)
    row_back = mm(dhid, w_in, NT)

    @pl.when(f == 0)
    def _():
        out_acc[...] = row_out
        back_acc[...] = row_back

    @pl.when(f > 0)
    def _():
        out_acc[...] += row_out
        back_acc[...] += row_back

    @pl.when(f == pl.num_programs(0) - 1)
    def _():
        put_rows(stage_ref, out_acc[...], 0, 0, images, images, groups)
        put_rows(stage_ref, back_acc[...], 1, 0, images, images, groups)
        pack_rows(stage_ref, back_ref)


def experts(packed, w_in, w_out, block):
    width, hidden = w_in.shape[1:]
    groups = packed.shape[0]
    rows = packed.shape[1] * LANES // (2 * width) * groups
    return pl.pallas_call(
        functools.partial(expert_body, rows // groups),
        grid=(hidden // block,),
        in_specs=[
            pl.BlockSpec(packed.shape, lambda f: (0, 0, 0)),
            pl.BlockSpec((1, width, block), lambda f: (0, 0, f)),
            pl.BlockSpec((1, block, width), lambda f: (0, f, 0)),
        ],
        out_specs=[
            pl.BlockSpec((rows, block), lambda f: (0, f)),
            pl.BlockSpec((rows, block), lambda f: (0, f)),
            pl.BlockSpec(packed.shape, lambda f: (0, 0, 0)),
        ],
        out_shape=[
            jax.ShapeDtypeStruct((rows, hidden), BF16),
            jax.ShapeDtypeStruct((rows, hidden), BF16),
            jax.ShapeDtypeStruct(packed.shape, BF16),
        ],
        scratch_shapes=[
            pltpu.VMEM((groups * packed.shape[1], LANES), F32),
            pltpu.VMEM((rows, width), BF16),
            pltpu.VMEM((rows, width), BF16),
            pltpu.VMEM((rows, width), F32),
            pltpu.VMEM((rows, width), F32),
        ],
        compiler_params=params(),
        name="experts",
    )(packed, w_in, w_out)


def logit_body(images, packed_ref, tokens_ref, grad_ref, disp_ref, comb_ref, lgrad_ref, sback_ref, router_ref,
               stage_ref, acc_ref):
    i = pl.program_id(0)
    slots = packed_ref.shape[0]

    @pl.when(i == 0)
    def _():
        stage_rows(packed_ref, stage_ref)

    slot_out = whole_rows(stage_ref, 0, i, 1, images, slots)
    slot_back = whole_rows(stage_ref, 1, i, 1, images, slots)
    sback_ref[0] = slot_back
    tok = tokens_ref[0]
    comb_dot = mm(slot_out, grad_ref[0], NT)
    disp_dot = mm(slot_back, tok, NT)
    combine, dispatch = comb_ref[0], disp_ref[0]
    comb_part = combine * (comb_dot - jnp.sum(combine * comb_dot, axis=0, keepdims=True))
    disp_part = dispatch * (disp_dot - jnp.sum(dispatch * disp_dot, axis=1, keepdims=True))
    lgrad = (comb_part + disp_part).astype(BF16)
    lgrad_ref[0] = lgrad
    part = mm(lgrad, tok, NN)

    @pl.when(i == 0)
    def _():
        acc_ref[...] = part

    @pl.when(i > 0)
    def _():
        acc_ref[...] += part

    @pl.when(i == images - 1)
    def _():
        router_ref[...] = acc_ref[...].astype(BF16)


def logit_grads(packed, tokens, out_grad, dispatch, combine):
    images, toks, width = tokens.shape
    slots = packed.shape[0]
    image = lambda i: (i, 0, 0)
    return pl.pallas_call(
        functools.partial(logit_body, images),
        grid=(images,),
        in_specs=[
            pl.BlockSpec(packed.shape, lambda i: (0, 0, 0)),
            pl.BlockSpec((1, toks, width), image),
            pl.BlockSpec((1, toks, width), image),
            pl.BlockSpec((1, slots, toks), image),
            pl.BlockSpec((1, slots, toks), image),
        ],
        out_specs=[
            pl.BlockSpec((1, slots, toks), image),
            pl.BlockSpec((1, slots, width), image),
            pl.BlockSpec((slots, width), lambda i: (0, 0)),
        ],
        out_shape=[
            jax.ShapeDtypeStruct((images, slots, toks), BF16),
            jax.ShapeDtypeStruct((images, slots, width), BF16),
            jax.ShapeDtypeStruct((slots, width), BF16),
        ],
        scratch_shapes=[
            pltpu.VMEM((slots * packed.shape[1], LANES), F32),
            pltpu.VMEM((slots, width), F32),
        ],
        compiler_params=params(),
        name="logit_grads",
    )(packed, tokens, out_grad, dispatch, combine)


def token_body(lgrad_ref, disp_ref, sback_ref, router_ref, out_ref):
    left = jnp.concatenate([lgrad_ref[0], disp_ref[0].astype(BF16)], axis=0)
    right = jnp.concatenate([router_ref[...], sback_ref[0]], axis=0)
    out_ref[0] = mm(left, right, TN).astype(BF16)


def token_grads(lgrad, dispatch, slot_back, router):
    images, slots, toks = lgrad.shape
    width = router.shape[1]
    image = lambda i: (i, 0, 0)
    return pl.pallas_call(
        token_body,
        grid=(images,),
        in_specs=[
            pl.BlockSpec((1, slots, toks), image),
            pl.BlockSpec((1, slots, toks), image),
            pl.BlockSpec((1, slots, width), image),
            pl.BlockSpec((slots, width), lambda i: (0, 0)),
        ],
        out_specs=pl.BlockSpec((1, toks, width), image),
        out_shape=jax.ShapeDtypeStruct((images, toks, width), BF16),
        compiler_params=params(),
        name="token_grads",
    )(lgrad, dispatch, slot_back, router)


def weight_body(images, start_ref, own_ref, peer_ref, w_in_ref, w_out_ref, act_ref, dhid_ref,
                gin_ref, gout_ref, stage_ref, in_ref, grad_ref):
    del start_ref
    f = pl.program_id(0)
    groups = own_ref.shape[0]
    rows = images * groups

    @pl.when(f == 0)
    def _():
        for part, packed_ref in enumerate((own_ref, peer_ref)):
            stage_rows(packed_ref, stage_ref)
            where = pl.ds(part * rows, rows)
            in_ref[where, :] = whole_rows(stage_ref, 0, 0, images, images, groups)
            grad_ref[where, :] = whole_rows(stage_ref, 1, 0, images, images, groups)

    act, slope = gelu_parts(mm(in_ref[rows:, :], w_in_ref[0], NN))
    dhid = (mm(grad_ref[rows:, :], w_out_ref[0], NT) * slope).astype(BF16)
    act = jnp.concatenate([act_ref[...], act.astype(BF16)], axis=0)
    dhid = jnp.concatenate([dhid_ref[...], dhid], axis=0)
    gin_ref[0] = mm(in_ref[...], dhid, TN).astype(BF16)
    gout_ref[0] = mm(act, grad_ref[...], TN).astype(BF16)


def weight_grads(start, own, peer, w_in, w_out, act, dhid, block, reps):
    width, hidden = w_in.shape[1], w_in.shape[2] // reps
    groups = own.shape[0]
    rows = own.shape[1] * LANES // (2 * width) * groups
    return pl.pallas_call(
        functools.partial(weight_body, rows // groups),
        grid_spec=pltpu.PrefetchScalarGridSpec(
            num_scalar_prefetch=1,
            grid=(hidden // block,),
            in_specs=[
                pl.BlockSpec(own.shape, lambda f, s: (0, 0, 0)),
                pl.BlockSpec(own.shape, lambda f, s: (0, 0, 0)),
                pl.BlockSpec((1, width, block), lambda f, s: (0, 0, s[0] + f)),
                pl.BlockSpec((1, block, width), lambda f, s: (0, s[0] + f, 0)),
                pl.BlockSpec((rows, block), lambda f, s: (0, s[0] + f)),
                pl.BlockSpec((rows, block), lambda f, s: (0, s[0] + f)),
            ],
            out_specs=[
                pl.BlockSpec((1, width, block), lambda f, s: (0, 0, f)),
                pl.BlockSpec((1, block, width), lambda f, s: (0, f, 0)),
            ],
            scratch_shapes=[
                pltpu.VMEM((groups * own.shape[1], LANES), F32),
                pltpu.VMEM((2 * rows, width), BF16),
                pltpu.VMEM((2 * rows, width), BF16),
            ],
        ),
        out_shape=[
            jax.ShapeDtypeStruct((1, width, hidden), BF16),
            jax.ShapeDtypeStruct((1, hidden, width), BF16),
        ],
        compiler_params=params(),
        name="weight_grads",
    )(start, own, peer, w_in, w_out, act, dhid)


def swap(value, axis):
    return lax.all_to_all(value, axis, split_axis=0, concat_axis=0, tiled=True)


def per_device(tokens, out_grad, router, w_in, w_out):
    reps = lax.axis_size("rep")
    devices = lax.axis_size("exp") * reps
    dispatch, combine, to_experts = gather_slots(tokens, out_grad, router)
    own = swap(to_experts, "exp")
    act, dhid, to_images = experts(own, w_in, w_out, 512)
    peer = lax.ppermute(own, "rep", [(i, i ^ 1) for i in range(reps)])
    back = swap(to_images, "exp")
    lgrad, slot_back, router_part = logit_grads(back, tokens, out_grad, dispatch, combine)
    shares = swap(router_part.reshape(devices, -1, 128), ("exp", "rep")).astype(F32)
    share = jnp.sum(shares, axis=0).astype(BF16)
    router_grad = swap(jnp.broadcast_to(share[None], shares.shape), ("exp", "rep"))
    router_grad = router_grad.reshape(router.shape).astype(F32)
    token_grad = token_grads(lgrad, dispatch, slot_back, router)
    block = 256
    start = (lax.axis_index("rep") * (w_in.shape[2] // reps // block)).astype(jnp.int32).reshape(1)
    grad_in, grad_out = weight_grads(start, own, peer, w_in, w_out, act, dhid, block, reps)
    return token_grad, grad_in, grad_out, router_grad


def solution(mesh):
    in_specs = (
        P(("exp", "rep"), None, None),
        P(("exp", "rep"), None, None),
        P(),
        P("exp", None, None),
        P("exp", None, None),
    )
    out_specs = (P(("exp", "rep"), None, None), P("exp", None, "rep"), P("exp", "rep", None), P())
    return jax.shard_map(
        per_device, mesh=mesh, in_specs=in_specs, out_specs=out_specs, check_vma=False
    )
```

```python
import functools

import jax
import jax.numpy as jnp
from jax import lax
from jax.experimental import pallas as pl
from jax.experimental.pallas import tpu as pltpu
from jax.sharding import PartitionSpec as P

BF16, F32 = jnp.bfloat16, jnp.float32
NN, NT, TN = ((1,), (0,)), ((1,), (1,)), ((0,), (0,))
VMEM_LIMIT = 56 * 2**20
LANES = 128
SUBLANES = 8
PITCH_PAD = 8


def mm(a, b, dims):
    return lax.dot_general(a, b, (dims, ((), ())), preferred_element_type=F32)


def params():
    return pltpu.CompilerParams(vmem_limit_bytes=VMEM_LIMIT)


def gelu_parts(hidden):
    cdf = 0.5 * (1.0 + lax.erf(hidden * 0.7071067811865476))
    density = jnp.exp(-0.5 * hidden * hidden) * 0.3989422804014327
    return hidden * cdf, cdf + hidden * density


def pitch_of(groups):
    return groups + PITCH_PAD


def stage_rows(packed_refs, stage_ref):
    rows = packed_refs[0].shape[1]
    pitch = stage_ref.shape[0] // rows
    first = 0
    for packed_ref in packed_refs:
        groups = packed_ref.shape[0]

        def body(g, carry, packed_ref=packed_ref, first=first):
            stage_ref[pl.ds(first + g, rows, stride=pitch), :] = packed_ref[g].astype(F32)
            return carry

        lax.fori_loop(0, groups, body, 0, unroll=8)
        first += groups


def pack_rows(stage_ref, packed_ref):
    groups, rows, _ = packed_ref.shape

    def body(g, carry):
        packed_ref[g] = stage_ref[pl.ds(g, rows, stride=pitch_of(groups)), :].astype(BF16)
        return carry

    lax.fori_loop(0, groups, body, 0, unroll=8)


def piece_rows(piece, which, image, images, groups):
    start = ((piece * 2 + which) * images + image) * pitch_of(groups)
    return pl.ds(start if isinstance(start, int) else pl.multiple_of(start, 8), groups)


def image_rows(stage_ref, which, image, images, groups):
    pieces = stage_ref.shape[0] // (2 * images * pitch_of(groups))
    parts = [stage_ref[piece_rows(p, which, image, images, groups), :] for p in range(pieces)]
    return jnp.concatenate([part.astype(BF16) for part in parts], axis=1)


def put_image(stage_ref, value, which, image, images, groups):
    for p in range(value.shape[1] // LANES):
        cols = value[:, p * LANES : (p + 1) * LANES]
        stage_ref[piece_rows(p, which, image, images, groups), :] = cols


def load_rows(stage_ref, row_ref, first, which, images, groups):
    for image in range(images):
        where = slice(first + image * groups, first + (image + 1) * groups)
        row_ref[where, :] = image_rows(stage_ref, which, image, images, groups)


def stage_shape(packed_shape):
    return pltpu.VMEM((pitch_of(packed_shape[0]) * packed_shape[1], LANES), F32)


def gather_body(images, tokens_ref, grad_ref, router_ref, disp_ref, comb_ref, packed_ref, stage_ref):
    i = pl.program_id(0)
    slots = router_ref.shape[0]
    each = tokens_ref.shape[0]
    for j in range(each):
        tok = tokens_ref[j]
        logits = mm(router_ref[...], tok, NT)
        d_exp = jnp.exp(logits - jnp.max(logits, axis=1, keepdims=True))
        dispatch = d_exp / jnp.sum(d_exp, axis=1, keepdims=True)
        c_exp = jnp.exp(logits - jnp.max(logits, axis=0, keepdims=True))
        combine = c_exp / jnp.sum(c_exp, axis=0, keepdims=True)
        disp_ref[j] = dispatch
        comb_ref[j] = combine
        slot_in = mm(dispatch.astype(BF16), tok, NN)
        slot_grad = mm(combine.astype(BF16), grad_ref[j], NN)
        put_image(stage_ref, slot_in, 0, i * each + j, images, slots)
        put_image(stage_ref, slot_grad, 1, i * each + j, images, slots)

    @pl.when(i == pl.num_programs(0) - 1)
    def _():
        pack_rows(stage_ref, packed_ref)


def gather_slots(tokens, out_grad, router, each):
    images, toks, width = tokens.shape
    slots = router.shape[0]
    packed = (slots, 2 * images * width // LANES, LANES)
    image = lambda i: (i, 0, 0)
    return pl.pallas_call(
        functools.partial(gather_body, images),
        grid=(images // each,),
        in_specs=[
            pl.BlockSpec((each, toks, width), image),
            pl.BlockSpec((each, toks, width), image),
            pl.BlockSpec((slots, width), lambda i: (0, 0)),
        ],
        out_specs=[
            pl.BlockSpec((each, slots, toks), image),
            pl.BlockSpec((each, slots, toks), image),
            pl.BlockSpec(packed, lambda i: (0, 0, 0)),
        ],
        out_shape=[
            jax.ShapeDtypeStruct((images, slots, toks), F32),
            jax.ShapeDtypeStruct((images, slots, toks), F32),
            jax.ShapeDtypeStruct(packed, BF16),
        ],
        scratch_shapes=[stage_shape(packed)],
        compiler_params=params(),
        name="gather_slots",
    )(tokens, out_grad, router)


def expert_body(images, packed_ref, w_in_ref, w_out_ref, act_ref, dhid_ref, back_ref, in_ref, grad_ref,
                stage_ref, out_acc, back_acc):
    f = pl.program_id(0)
    groups = packed_ref.shape[0]

    @pl.when(f == 0)
    def _():
        stage_rows((packed_ref,), stage_ref)
        load_rows(stage_ref, in_ref, 0, 0, images, groups)
        load_rows(stage_ref, grad_ref, 0, 1, images, groups)
        out_acc[...] = jnp.zeros_like(out_acc)
        back_acc[...] = jnp.zeros_like(back_acc)

    w_in, w_out = w_in_ref[0], w_out_ref[0]
    act, slope = gelu_parts(mm(in_ref[...], w_in, NN))
    act = act.astype(BF16)
    act_ref[...] = act
    dhid = (mm(grad_ref[...], w_out, NT) * slope).astype(BF16)
    dhid_ref[...] = dhid
    out_acc[...] += mm(act, w_out, NN)
    back_acc[...] += mm(dhid, w_in, NT)

    @pl.when(f == pl.num_programs(0) - 1)
    def _():
        for image in range(images):
            where = slice(image * groups, (image + 1) * groups)
            put_image(stage_ref, out_acc[where, :], 0, image, images, groups)
            put_image(stage_ref, back_acc[where, :], 1, image, images, groups)
        pack_rows(stage_ref, back_ref)


def experts(packed, w_in, w_out, block):
    width, hidden = w_in.shape[1:]
    groups = packed.shape[0]
    rows = packed.shape[1] * LANES // (2 * width) * groups
    return pl.pallas_call(
        functools.partial(expert_body, rows // groups),
        grid=(hidden // block,),
        in_specs=[
            pl.BlockSpec(packed.shape, lambda f: (0, 0, 0)),
            pl.BlockSpec((1, width, block), lambda f: (0, 0, f)),
            pl.BlockSpec((1, block, width), lambda f: (0, f, 0)),
        ],
        out_specs=[
            pl.BlockSpec((rows, block), lambda f: (0, f)),
            pl.BlockSpec((rows, block), lambda f: (0, f)),
            pl.BlockSpec(packed.shape, lambda f: (0, 0, 0)),
            pl.BlockSpec((rows, width), lambda f: (0, 0)),
            pl.BlockSpec((rows, width), lambda f: (0, 0)),
        ],
        out_shape=[
            jax.ShapeDtypeStruct((rows, hidden), BF16),
            jax.ShapeDtypeStruct((rows, hidden), BF16),
            jax.ShapeDtypeStruct(packed.shape, BF16),
            jax.ShapeDtypeStruct((rows, width), BF16),
            jax.ShapeDtypeStruct((rows, width), BF16),
        ],
        scratch_shapes=[
            stage_shape(packed.shape),
            pltpu.VMEM((rows, width), F32),
            pltpu.VMEM((rows, width), F32),
        ],
        compiler_params=params(),
        name="experts",
    )(packed, w_in, w_out)


def logit_body(images, packed_ref, tokens_ref, grad_ref, disp_ref, comb_ref, lgrad_ref, sback_ref, router_ref,
               stage_ref, acc_ref):
    i = pl.program_id(0)
    slots = packed_ref.shape[0]

    @pl.when(i == 0)
    def _():
        stage_rows((packed_ref,), stage_ref)
        acc_ref[...] = jnp.zeros_like(acc_ref)

    each = tokens_ref.shape[0]
    for j in range(each):
        slot_out = image_rows(stage_ref, 0, i * each + j, images, slots)
        slot_back = image_rows(stage_ref, 1, i * each + j, images, slots)
        sback_ref[j] = slot_back
        tok = tokens_ref[j]
        comb_dot = mm(slot_out, grad_ref[j], NT)
        disp_dot = mm(slot_back, tok, NT)
        combine, dispatch = comb_ref[j], disp_ref[j]
        comb_part = combine * (comb_dot - jnp.sum(combine * comb_dot, axis=0, keepdims=True))
        disp_part = dispatch * (disp_dot - jnp.sum(dispatch * disp_dot, axis=1, keepdims=True))
        lgrad = (comb_part + disp_part).astype(BF16)
        lgrad_ref[j] = lgrad
        acc_ref[...] += mm(lgrad, tok, NN)

    @pl.when(i == pl.num_programs(0) - 1)
    def _():
        tiles = 0
        for first in range(0, slots, SUBLANES):
            for col in range(0, acc_ref.shape[1], LANES):
                tile = acc_ref[first : first + SUBLANES, col : col + LANES]
                router_ref[tiles] = tile.astype(BF16)
                tiles += 1
        router_ref[tiles:] = jnp.zeros((router_ref.shape[0] - tiles, SUBLANES, LANES), BF16)


def logit_grads(packed, tokens, out_grad, dispatch, combine, devices, each):
    images, toks, width = tokens.shape
    slots = packed.shape[0]
    assert slots * width <= devices * SUBLANES * LANES
    image = lambda i: (i, 0, 0)
    return pl.pallas_call(
        functools.partial(logit_body, images),
        grid=(images // each,),
        in_specs=[
            pl.BlockSpec(packed.shape, lambda i: (0, 0, 0)),
            pl.BlockSpec((each, toks, width), image),
            pl.BlockSpec((each, toks, width), image),
            pl.BlockSpec((each, slots, toks), image),
            pl.BlockSpec((each, slots, toks), image),
        ],
        out_specs=[
            pl.BlockSpec((each, slots, toks), image),
            pl.BlockSpec((each, slots, width), image),
            pl.BlockSpec((devices, SUBLANES, LANES), lambda i: (0, 0, 0)),
        ],
        out_shape=[
            jax.ShapeDtypeStruct((images, slots, toks), BF16),
            jax.ShapeDtypeStruct((images, slots, width), BF16),
            jax.ShapeDtypeStruct((devices, SUBLANES, LANES), BF16),
        ],
        scratch_shapes=[
            stage_shape(packed.shape),
            pltpu.VMEM((slots, width), F32),
        ],
        compiler_params=params(),
        name="logit_grads",
    )(packed, tokens, out_grad, dispatch, combine)


def token_body(lgrad_ref, disp_ref, sback_ref, router_ref, out_ref):
    for j in range(out_ref.shape[0]):
        left = jnp.concatenate([lgrad_ref[j], disp_ref[j].astype(BF16)], axis=0)
        right = jnp.concatenate([router_ref[...], sback_ref[j]], axis=0)
        out_ref[j] = mm(left, right, TN).astype(BF16)


def token_grads(lgrad, dispatch, slot_back, router, each):
    images, slots, toks = lgrad.shape
    width = router.shape[1]
    image = lambda i: (i, 0, 0)
    return pl.pallas_call(
        token_body,
        grid=(images // each,),
        in_specs=[
            pl.BlockSpec((each, slots, toks), image),
            pl.BlockSpec((each, slots, toks), image),
            pl.BlockSpec((each, slots, width), image),
            pl.BlockSpec((slots, width), lambda i: (0, 0)),
        ],
        out_specs=pl.BlockSpec((each, toks, width), image),
        out_shape=jax.ShapeDtypeStruct((images, toks, width), BF16),
        compiler_params=params(),
        name="token_grads",
    )(lgrad, dispatch, slot_back, router)


def weight_body(images, n_packed, n_own, n_first, start_ref, *refs):
    del start_ref
    packed_refs, refs = refs[:n_packed], refs[n_packed:]
    (w_in_ref, w_out_ref), refs = refs[:2], refs[2:]
    own_refs, refs = refs[:n_own], refs[n_own:]
    first_refs, refs = refs[:n_first], refs[n_first:]
    gin_ref, gout_ref, stage_ref, in_ref, grad_ref = refs
    groups = sum(packed_ref.shape[0] for packed_ref in packed_refs)

    @pl.when(pl.program_id(0) == 0)
    def _():
        stage_rows(packed_refs, stage_ref)
        load_rows(stage_ref, in_ref, 0, 0, images, groups)
        load_rows(stage_ref, grad_ref, 0, 1, images, groups)

    act, slope = gelu_parts(mm(in_ref[...], w_in_ref[0], NN))
    dhid = (mm(grad_ref[...], w_out_ref[0], NT) * slope).astype(BF16)
    gin = mm(in_ref[...], dhid, TN)
    gout = mm(act.astype(BF16), grad_ref[...], TN)
    if n_own:
        own_in_ref, own_grad_ref, own_act_ref, own_dhid_ref = own_refs
        gin += mm(own_in_ref[...], own_dhid_ref[...], TN)
        gout += mm(own_act_ref[...], own_grad_ref[...], TN)
    if n_first:
        gin += first_refs[0][0].astype(F32)
        gout += first_refs[1][0].astype(F32)
    gin_ref[0] = gin.astype(gin_ref.dtype)
    gout_ref[0] = gout.astype(gout_ref.dtype)


def weight_grads(start, packed, w_in, w_out, own, first, block, reps, dtype, name):
    width, hidden = w_in.shape[1], w_in.shape[2] // reps
    groups, pieces = sum(p.shape[0] for p in packed), packed[0].shape[1]
    images = pieces * LANES // (2 * width)
    rows = images * groups
    in_specs = [pl.BlockSpec(v.shape, lambda f, s: (0, 0, 0)) for v in packed]
    in_specs += [
        pl.BlockSpec((1, width, block), lambda f, s: (0, 0, s[0] + f)),
        pl.BlockSpec((1, block, width), lambda f, s: (0, s[0] + f, 0)),
    ]
    if own:
        own_rows = own[0].shape[0]
        in_specs += [pl.BlockSpec((own_rows, width), lambda f, s: (0, 0))] * 2
        in_specs += [pl.BlockSpec((own_rows, block), lambda f, s: (0, s[0] + f))] * 2
    outs = [
        pl.BlockSpec((1, width, block), lambda f, s: (0, 0, f)),
        pl.BlockSpec((1, block, width), lambda f, s: (0, f, 0)),
    ]
    if first:
        in_specs += outs
    return pl.pallas_call(
        functools.partial(weight_body, images, len(packed), len(own), len(first)),
        grid_spec=pltpu.PrefetchScalarGridSpec(
            num_scalar_prefetch=1,
            grid=(hidden // block,),
            in_specs=in_specs,
            out_specs=outs,
            scratch_shapes=[
                stage_shape((groups, pieces)),
                pltpu.VMEM((rows, width), BF16),
                pltpu.VMEM((rows, width), BF16),
            ],
        ),
        out_shape=[
            jax.ShapeDtypeStruct((1, width, hidden), dtype),
            jax.ShapeDtypeStruct((1, hidden, width), dtype),
        ],
        compiler_params=params(),
        name=name,
    )(start, *packed, w_in, w_out, *own, *first)


def swap(value, axis):
    return lax.all_to_all(value, axis, split_axis=0, concat_axis=0, tiled=True)


def per_device(tokens, out_grad, router, w_in, w_out):
    reps = lax.axis_size("rep")
    devices = lax.axis_size("exp") * reps
    slots, width = router.shape
    dispatch, combine, to_experts = gather_slots(tokens, out_grad, router, 3)
    own = swap(to_experts, "exp")
    act, dhid, to_images, row_in, row_grad = experts(own, w_in, w_out, 512)
    hidden, block = w_in.shape[2] // reps, 640
    start = (lax.axis_index("rep") * (hidden // block)).astype(jnp.int32).reshape(1)
    pairs = [(i, i ^ 1) for i in range(reps)]
    cut = own.shape[0] * 3 // 8
    peer_first = lax.ppermute(own[:cut], "rep", pairs)
    peer_last = lax.ppermute(own[cut:], "rep", pairs)
    to_images, peer_first = lax.optimization_barrier((to_images, peer_first))
    back = swap(to_images, "exp")
    own_rows = (row_in, row_grad, act, dhid)
    first = weight_grads(start, [peer_first], w_in, w_out, own_rows, (), block, reps, F32, "weight_first")
    back, first = lax.optimization_barrier((back, first))
    lgrad, slot_back, tiles = logit_grads(back, tokens, out_grad, dispatch, combine, devices, 2)
    start, tiles = lax.optimization_barrier((start, tiles))
    shares = swap(tiles, ("exp", "rep")).astype(F32)
    share = jnp.sum(shares, axis=0).astype(BF16)
    token_grad = token_grads(lgrad, dispatch, slot_back, router, 3)
    share, token_grad = lax.optimization_barrier((share, token_grad))
    start, share = lax.optimization_barrier((start, share))
    tiles = swap(jnp.broadcast_to(share[None], shares.shape), ("exp", "rep"))
    tiles = tiles[: slots * width // (SUBLANES * LANES)].reshape(slots // SUBLANES, width // LANES, SUBLANES, LANES)
    router_grad = tiles.transpose(0, 2, 1, 3).reshape(slots, width).astype(F32)
    grad_in, grad_out = weight_grads(start, [peer_last], w_in, w_out, (), first, block, reps, BF16, "weight_last")
    return token_grad, grad_in, grad_out, router_grad


def solution(mesh):
    in_specs = (
        P(("exp", "rep"), None, None),
        P(("exp", "rep"), None, None),
        P(),
        P("exp", None, None),
        P("exp", None, None),
    )
    out_specs = (P(("exp", "rep"), None, None), P("exp", None, "rep"), P("exp", "rep", None), P())
    return jax.shard_map(
        per_device, mesh=mesh, in_specs=in_specs, out_specs=out_specs, check_vma=False
    )
```

```python
import functools

import jax
import jax.numpy as jnp
from jax import lax
from jax.experimental import pallas as pl
from jax.experimental.pallas import tpu as pltpu
from jax.sharding import PartitionSpec as P

BF16, F32 = jnp.bfloat16, jnp.float32
NN, NT, TN = ((1,), (0,)), ((1,), (1,)), ((0,), (0,))
VMEM_LIMIT = 56 * 2**20
LANES = 128
SUBLANES = 8
PITCH_PAD = 8


def mm(a, b, dims):
    return lax.dot_general(a, b, (dims, ((), ())), preferred_element_type=F32)


def params(limit=VMEM_LIMIT):
    return pltpu.CompilerParams(vmem_limit_bytes=limit)


def gelu_parts(hidden):
    cdf = 0.5 * (1.0 + lax.erf(hidden * 0.7071067811865476))
    density = jnp.exp(-0.5 * hidden * hidden) * 0.3989422804014327
    return hidden * cdf, cdf + hidden * density


def pitch_of(groups):
    return groups + PITCH_PAD


def stage_rows(packed_refs, stage_ref):
    rows = packed_refs[0].shape[1]
    pitch = stage_ref.shape[0] // rows
    first = 0
    for packed_ref in packed_refs:
        groups = packed_ref.shape[0]

        def body(g, carry, packed_ref=packed_ref, first=first):
            stage_ref[pl.ds(first + g, rows, stride=pitch), :] = packed_ref[g].astype(F32)
            return carry

        lax.fori_loop(0, groups, body, 0, unroll=8)
        first += groups


def pack_rows(stage_ref, packed_ref):
    groups, rows, _ = packed_ref.shape

    def body(g, carry):
        packed_ref[g] = stage_ref[pl.ds(g, rows, stride=pitch_of(groups)), :].astype(BF16)
        return carry

    lax.fori_loop(0, groups, body, 0, unroll=8)


def piece_rows(piece, which, image, images, groups):
    start = ((piece * 2 + which) * images + image) * pitch_of(groups)
    return pl.ds(start if isinstance(start, int) else pl.multiple_of(start, 8), groups)


def image_rows(stage_ref, which, image, images, groups):
    pieces = stage_ref.shape[0] // (2 * images * pitch_of(groups))
    parts = [stage_ref[piece_rows(p, which, image, images, groups), :] for p in range(pieces)]
    return jnp.concatenate([part.astype(BF16) for part in parts], axis=1)


def put_image(stage_ref, value, which, image, images, groups):
    for p in range(value.shape[1] // LANES):
        cols = value[:, p * LANES : (p + 1) * LANES]
        stage_ref[piece_rows(p, which, image, images, groups), :] = cols


def load_rows(stage_ref, row_ref, first, which, images, groups):
    for image in range(images):
        where = slice(first + image * groups, first + (image + 1) * groups)
        row_ref[where, :] = image_rows(stage_ref, which, image, images, groups)


def stage_shape(packed_shape):
    return pltpu.VMEM((pitch_of(packed_shape[0]) * (packed_shape[1] + 1), LANES), F32)


def gather_body(images, tokens_ref, grad_ref, router_ref, disp_ref, comb_ref, packed_ref, stage_ref):
    i = pl.program_id(0)
    slots = router_ref.shape[0]
    each = tokens_ref.shape[0]
    for j in range(each):
        tok = tokens_ref[j]
        logits = mm(router_ref[...], tok, NT)
        d_exp = jnp.exp(logits - jnp.max(logits, axis=1, keepdims=True))
        dispatch = d_exp / jnp.sum(d_exp, axis=1, keepdims=True)
        c_exp = jnp.exp(logits - jnp.max(logits, axis=0, keepdims=True))
        combine = c_exp / jnp.sum(c_exp, axis=0, keepdims=True)
        disp_ref[j] = dispatch
        comb_ref[j] = combine
        slot_in = mm(dispatch.astype(BF16), tok, NN)
        slot_grad = mm(combine.astype(BF16), grad_ref[j], NN)
        put_image(stage_ref, slot_in, 0, i * each + j, images, slots)
        put_image(stage_ref, slot_grad, 1, i * each + j, images, slots)

    @pl.when(i == pl.num_programs(0) - 1)
    def _():
        pack_rows(stage_ref, packed_ref)


def gather_slots(tokens, out_grad, router, each):
    images, toks, width = tokens.shape
    slots = router.shape[0]
    packed = (slots, 2 * images * width // LANES, LANES)
    image = lambda i: (i, 0, 0)
    return pl.pallas_call(
        functools.partial(gather_body, images),
        grid=(images // each,),
        in_specs=[
            pl.BlockSpec((each, toks, width), image),
            pl.BlockSpec((each, toks, width), image),
            pl.BlockSpec((slots, width), lambda i: (0, 0)),
        ],
        out_specs=[
            pl.BlockSpec((each, slots, toks), image),
            pl.BlockSpec((each, slots, toks), image),
            pl.BlockSpec(packed, lambda i: (0, 0, 0)),
        ],
        out_shape=[
            jax.ShapeDtypeStruct((images, slots, toks), F32),
            jax.ShapeDtypeStruct((images, slots, toks), F32),
            jax.ShapeDtypeStruct(packed, BF16),
        ],
        scratch_shapes=[stage_shape(packed)],
        compiler_params=params(),
        name="gather_slots",
    )(tokens, out_grad, router)


def expert_body(images, packed_ref, w_in_ref, w_out_ref, act_ref, dhid_ref, back_ref,
                stage_ref, in_ref, grad_ref, out_acc, back_acc):
    f = pl.program_id(0)
    groups = packed_ref.shape[0]

    @pl.when(f == 0)
    def _():
        stage_rows((packed_ref,), stage_ref)
        load_rows(stage_ref, in_ref, 0, 0, images, groups)
        load_rows(stage_ref, grad_ref, 0, 1, images, groups)
        out_acc[...] = jnp.zeros_like(out_acc)
        back_acc[...] = jnp.zeros_like(back_acc)

    w_in, w_out = w_in_ref[0], w_out_ref[0]
    act, slope = gelu_parts(mm(in_ref[...], w_in, NN))
    act = act.astype(BF16)
    act_ref[...] = act
    dhid = (mm(grad_ref[...], w_out, NT) * slope).astype(BF16)
    dhid_ref[...] = dhid
    out_acc[...] += mm(act, w_out, NN)
    back_acc[...] += mm(dhid, w_in, NT)

    @pl.when(f == pl.num_programs(0) - 1)
    def _():
        for image in range(images):
            where = slice(image * groups, (image + 1) * groups)
            put_image(stage_ref, out_acc[where, :], 0, image, images, groups)
            put_image(stage_ref, back_acc[where, :], 1, image, images, groups)
        pack_rows(stage_ref, back_ref)


def experts(packed, w_in, w_out, block):
    width, hidden = w_in.shape[1:]
    groups = packed.shape[0]
    rows = packed.shape[1] * LANES // (2 * width) * groups
    return pl.pallas_call(
        functools.partial(expert_body, rows // groups),
        grid=(hidden // block,),
        in_specs=[
            pl.BlockSpec(packed.shape, lambda f: (0, 0, 0)),
            pl.BlockSpec((1, width, block), lambda f: (0, 0, f)),
            pl.BlockSpec((1, block, width), lambda f: (0, f, 0)),
        ],
        out_specs=[
            pl.BlockSpec((rows, block), lambda f: (0, f)),
            pl.BlockSpec((rows, block), lambda f: (0, f)),
            pl.BlockSpec(packed.shape, lambda f: (0, 0, 0)),
        ],
        out_shape=[
            jax.ShapeDtypeStruct((rows, hidden), BF16),
            jax.ShapeDtypeStruct((rows, hidden), BF16),
            jax.ShapeDtypeStruct(packed.shape, BF16),
        ],
        scratch_shapes=[
            stage_shape(packed.shape),
            pltpu.VMEM((rows, width), BF16),
            pltpu.VMEM((rows, width), BF16),
            pltpu.VMEM((rows, width), F32),
            pltpu.VMEM((rows, width), F32),
        ],
        compiler_params=params(),
        name="experts",
    )(packed, w_in, w_out)


def logit_body(images, packed_ref, tokens_ref, grad_ref, disp_ref, comb_ref, lgrad_ref, sback_ref, router_ref,
               stage_ref, acc_ref):
    i = pl.program_id(0)
    slots = packed_ref.shape[0]

    @pl.when(i == 0)
    def _():
        stage_rows((packed_ref,), stage_ref)
        acc_ref[...] = jnp.zeros_like(acc_ref)

    each = tokens_ref.shape[0]
    for j in range(each):
        slot_out = image_rows(stage_ref, 0, i * each + j, images, slots)
        slot_back = image_rows(stage_ref, 1, i * each + j, images, slots)
        sback_ref[j] = slot_back
        tok = tokens_ref[j]
        comb_dot = mm(slot_out, grad_ref[j], NT)
        disp_dot = mm(slot_back, tok, NT)
        combine, dispatch = comb_ref[j], disp_ref[j]
        comb_part = combine * (comb_dot - jnp.sum(combine * comb_dot, axis=0, keepdims=True))
        disp_part = dispatch * (disp_dot - jnp.sum(dispatch * disp_dot, axis=1, keepdims=True))
        lgrad = (comb_part + disp_part).astype(BF16)
        lgrad_ref[j] = lgrad
        acc_ref[...] += mm(lgrad, tok, NN)

    @pl.when(i == pl.num_programs(0) - 1)
    def _():
        tiles = 0
        for first in range(0, slots, SUBLANES):
            for col in range(0, acc_ref.shape[1], LANES):
                tile = acc_ref[first : first + SUBLANES, col : col + LANES]
                router_ref[tiles] = tile.astype(BF16)
                tiles += 1
        router_ref[tiles:] = jnp.zeros((router_ref.shape[0] - tiles, SUBLANES, LANES), BF16)


def logit_grads(packed, tokens, out_grad, dispatch, combine, devices, each):
    images, toks, width = tokens.shape
    slots = packed.shape[0]
    assert slots * width <= devices * SUBLANES * LANES
    image = lambda i: (i, 0, 0)
    return pl.pallas_call(
        functools.partial(logit_body, images),
        grid=(images // each,),
        in_specs=[
            pl.BlockSpec(packed.shape, lambda i: (0, 0, 0)),
            pl.BlockSpec((each, toks, width), image),
            pl.BlockSpec((each, toks, width), image),
            pl.BlockSpec((each, slots, toks), image),
            pl.BlockSpec((each, slots, toks), image),
        ],
        out_specs=[
            pl.BlockSpec((each, slots, toks), image),
            pl.BlockSpec((each, slots, width), image),
            pl.BlockSpec((devices, SUBLANES, LANES), lambda i: (0, 0, 0)),
        ],
        out_shape=[
            jax.ShapeDtypeStruct((images, slots, toks), BF16),
            jax.ShapeDtypeStruct((images, slots, width), BF16),
            jax.ShapeDtypeStruct((devices, SUBLANES, LANES), BF16),
        ],
        scratch_shapes=[
            stage_shape(packed.shape),
            pltpu.VMEM((slots, width), F32),
        ],
        compiler_params=params(),
        name="logit_grads",
    )(packed, tokens, out_grad, dispatch, combine)


def token_body(lgrad_ref, disp_ref, sback_ref, router_ref, out_ref):
    for j in range(out_ref.shape[0]):
        left = jnp.concatenate([lgrad_ref[j], disp_ref[j].astype(BF16)], axis=0)
        right = jnp.concatenate([router_ref[...], sback_ref[j]], axis=0)
        out_ref[j] = mm(left, right, TN).astype(BF16)


def token_grads(lgrad, dispatch, slot_back, router, each):
    images, slots, toks = lgrad.shape
    width = router.shape[1]
    image = lambda i: (i, 0, 0)
    return pl.pallas_call(
        token_body,
        grid=(images // each,),
        in_specs=[
            pl.BlockSpec((each, slots, toks), image),
            pl.BlockSpec((each, slots, toks), image),
            pl.BlockSpec((each, slots, width), image),
            pl.BlockSpec((slots, width), lambda i: (0, 0)),
        ],
        out_specs=pl.BlockSpec((each, toks, width), image),
        out_shape=jax.ShapeDtypeStruct((images, toks, width), BF16),
        compiler_params=params(60 * 2**20),
        name="token_grads",
    )(lgrad, dispatch, slot_back, router)


def weight_body(images, n_packed, n_own, n_first, start_ref, *refs):
    del start_ref
    packed_refs, refs = refs[:n_packed], refs[n_packed:]
    (w_in_ref, w_out_ref), refs = refs[:2], refs[2:]
    own_refs, refs = refs[:n_own], refs[n_own:]
    first_refs, refs = refs[:n_first], refs[n_first:]
    gin_ref, gout_ref, stage_ref, in_ref, grad_ref = refs[:5]
    groups = sum(packed_ref.shape[0] for packed_ref in packed_refs)

    @pl.when(pl.program_id(0) == 0)
    def _():
        stage_rows(packed_refs, stage_ref)
        load_rows(stage_ref, in_ref, 0, 0, images, groups)
        load_rows(stage_ref, grad_ref, 0, 1, images, groups)
        if n_own:
            own_stage_ref, own_in_ref, own_grad_ref = refs[5:]
            own_groups = own_refs[0].shape[0]
            stage_rows(own_refs[:1], own_stage_ref)
            load_rows(own_stage_ref, own_in_ref, 0, 0, images, own_groups)
            load_rows(own_stage_ref, own_grad_ref, 0, 1, images, own_groups)

    act, slope = gelu_parts(mm(in_ref[...], w_in_ref[0], NN))
    dhid = (mm(grad_ref[...], w_out_ref[0], NT) * slope).astype(BF16)
    gin = mm(in_ref[...], dhid, TN)
    gout = mm(act.astype(BF16), grad_ref[...], TN)
    if n_own:
        own_in_ref, own_grad_ref = refs[6:]
        _, own_act_ref, own_dhid_ref = own_refs
        gin += mm(own_in_ref[...], own_dhid_ref[...], TN)
        gout += mm(own_act_ref[...], own_grad_ref[...], TN)
    if n_first:
        gin += first_refs[0][0].astype(F32)
        gout += first_refs[1][0].astype(F32)
    gin_ref[0] = gin.astype(gin_ref.dtype)
    gout_ref[0] = gout.astype(gout_ref.dtype)


def weight_grads(start, packed, w_in, w_out, own, first, block, reps, dtype, name):
    width, hidden = w_in.shape[1], w_in.shape[2] // reps
    groups, pieces = sum(p.shape[0] for p in packed), packed[0].shape[1]
    images = pieces * LANES // (2 * width)
    rows = images * groups
    in_specs = [pl.BlockSpec(v.shape, lambda f, s: (0, 0, 0)) for v in packed]
    in_specs += [
        pl.BlockSpec((1, width, block), lambda f, s: (0, 0, s[0] + f)),
        pl.BlockSpec((1, block, width), lambda f, s: (0, s[0] + f, 0)),
    ]
    if own:
        own_rows = own[1].shape[0]
        in_specs += [pl.BlockSpec(own[0].shape, lambda f, s: (0, 0, 0))]
        in_specs += [pl.BlockSpec((own_rows, block), lambda f, s: (0, s[0] + f))] * 2
    outs = [
        pl.BlockSpec((1, width, block), lambda f, s: (0, 0, f)),
        pl.BlockSpec((1, block, width), lambda f, s: (0, f, 0)),
    ]
    if first:
        in_specs += outs
    scratch = [stage_shape((groups, pieces)), pltpu.VMEM((rows, width), BF16), pltpu.VMEM((rows, width), BF16)]
    if own:
        scratch += [stage_shape(own[0].shape)] + [pltpu.VMEM((own_rows, width), BF16)] * 2
    return pl.pallas_call(
        functools.partial(weight_body, images, len(packed), len(own), len(first)),
        grid_spec=pltpu.PrefetchScalarGridSpec(
            num_scalar_prefetch=1,
            grid=(hidden // block,),
            in_specs=in_specs,
            out_specs=outs,
            scratch_shapes=scratch,
        ),
        out_shape=[
            jax.ShapeDtypeStruct((1, width, hidden), dtype),
            jax.ShapeDtypeStruct((1, hidden, width), dtype),
        ],
        compiler_params=params(),
        name=name,
    )(start, *packed, w_in, w_out, *own, *first)


def swap(value, axis):
    return lax.all_to_all(value, axis, split_axis=0, concat_axis=0, tiled=True)


def per_device(tokens, out_grad, router, w_in, w_out):
    reps = lax.axis_size("rep")
    devices = lax.axis_size("exp") * reps
    slots, width = router.shape
    dispatch, combine, to_experts = gather_slots(tokens, out_grad, router, 3)
    own = swap(to_experts, "exp")
    act, dhid, to_images = experts(own, w_in, w_out, 512)
    hidden, block = w_in.shape[2] // reps, 640
    start = (lax.axis_index("rep") * (hidden // block)).astype(jnp.int32).reshape(1)
    pairs = [(i, i ^ 1) for i in range(reps)]
    cut = own.shape[0] * 7 // 16
    peer_first = lax.ppermute(own[:cut], "rep", pairs)
    peer_last = lax.ppermute(own[cut:], "rep", pairs)
    to_images, peer_first = lax.optimization_barrier((to_images, peer_first))
    back = swap(to_images, "exp")
    first = weight_grads(start, [peer_first], w_in, w_out, (own, act, dhid), (), block, reps, BF16, "weight_first")
    back, first = lax.optimization_barrier((back, first))
    lgrad, slot_back, tiles = logit_grads(back, tokens, out_grad, dispatch, combine, devices, 2)
    start, tiles = lax.optimization_barrier((start, tiles))
    shares = swap(tiles, ("exp", "rep")).astype(F32)
    share = jnp.sum(shares, axis=0).astype(BF16)
    token_grad = token_grads(lgrad, dispatch, slot_back, router, 3)
    share, token_grad = lax.optimization_barrier((share, token_grad))
    start, share = lax.optimization_barrier((start, share))
    tiles = swap(jnp.broadcast_to(share[None], shares.shape), ("exp", "rep"))
    tiles = tiles[: slots * width // (SUBLANES * LANES)].reshape(slots // SUBLANES, width // LANES, SUBLANES, LANES)
    router_grad = tiles.transpose(0, 2, 1, 3).reshape(slots, width).astype(F32)
    grad_in, grad_out = weight_grads(start, [peer_last], w_in, w_out, (), first, block, reps, BF16, "weight_last")
    return token_grad, grad_in, grad_out, router_grad


def solution(mesh):
    in_specs = (
        P(("exp", "rep"), None, None),
        P(("exp", "rep"), None, None),
        P(),
        P("exp", None, None),
        P("exp", None, None),
    )
    out_specs = (P(("exp", "rep"), None, None), P("exp", None, "rep"), P("exp", "rep", None), P())
    return jax.shard_map(
        per_device, mesh=mesh, in_specs=in_specs, out_specs=out_specs, check_vma=False
    )
```

```python
import functools

import jax
import jax.numpy as jnp
from jax import lax
from jax.experimental import pallas as pl
from jax.experimental.pallas import tpu as pltpu
from jax.sharding import PartitionSpec as P

BF16, F32 = jnp.bfloat16, jnp.float32
NN, NT, TN = ((1,), (0,)), ((1,), (1,)), ((0,), (0,))
VMEM_LIMIT = 56 * 2**20
LANES = 128
SUBLANES = 8
PITCH_PAD = 8


def mm(a, b, dims):
    return lax.dot_general(a, b, (dims, ((), ())), preferred_element_type=F32)


def params(limit=VMEM_LIMIT):
    return pltpu.CompilerParams(vmem_limit_bytes=limit)


def gelu_parts(hidden):
    cdf = 0.5 * (1.0 + lax.erf(hidden * 0.7071067811865476))
    density = jnp.exp(-0.5 * hidden * hidden) * 0.3989422804014327
    return hidden * cdf, cdf + hidden * density


def pitch_of(groups):
    return groups + PITCH_PAD


def stage_rows(packed_refs, stage_ref):
    rows = packed_refs[0].shape[1]
    pitch = stage_ref.shape[0] // rows
    first = 0
    for packed_ref in packed_refs:
        groups = packed_ref.shape[0]

        def body(g, carry, packed_ref=packed_ref, first=first):
            stage_ref[pl.ds(first + g, rows, stride=pitch), :] = packed_ref[g].astype(F32)
            return carry

        lax.fori_loop(0, groups, body, 0, unroll=8)
        first += groups


def pack_rows(stage_ref, packed_ref):
    groups, rows, _ = packed_ref.shape

    def body(g, carry):
        packed_ref[g] = stage_ref[pl.ds(g, rows, stride=pitch_of(groups)), :].astype(BF16)
        return carry

    lax.fori_loop(0, groups, body, 0, unroll=8)


def piece_rows(piece, which, image, images, groups):
    start = ((piece * 2 + which) * images + image) * pitch_of(groups)
    return pl.ds(start if isinstance(start, int) else pl.multiple_of(start, 8), groups)


def image_rows(stage_ref, which, image, images, groups):
    pieces = stage_ref.shape[0] // (2 * images * pitch_of(groups))
    parts = [stage_ref[piece_rows(p, which, image, images, groups), :] for p in range(pieces)]
    return jnp.concatenate([part.astype(BF16) for part in parts], axis=1)


def put_image(stage_ref, value, which, image, images, groups):
    for p in range(value.shape[1] // LANES):
        cols = value[:, p * LANES : (p + 1) * LANES]
        stage_ref[piece_rows(p, which, image, images, groups), :] = cols


def load_rows(stage_ref, row_ref, first, which, images, groups):
    for image in range(images):
        where = slice(first + image * groups, first + (image + 1) * groups)
        row_ref[where, :] = image_rows(stage_ref, which, image, images, groups)


def stage_shape(packed_shape):
    return pltpu.VMEM((pitch_of(packed_shape[0]) * (packed_shape[1] + 1), LANES), F32)


def gather_body(images, tokens_ref, grad_ref, router_ref, disp_ref, comb_ref, packed_ref, stage_ref):
    i = pl.program_id(0)
    slots = router_ref.shape[0]
    each = tokens_ref.shape[0]
    for j in range(each):
        tok = tokens_ref[j]
        logits = mm(router_ref[...], tok, NT)
        d_exp = jnp.exp(logits - jnp.max(logits, axis=1, keepdims=True))
        dispatch = d_exp / jnp.sum(d_exp, axis=1, keepdims=True)
        c_exp = jnp.exp(logits - jnp.max(logits, axis=0, keepdims=True))
        combine = c_exp / jnp.sum(c_exp, axis=0, keepdims=True)
        disp_ref[j] = dispatch
        comb_ref[j] = combine
        slot_in = mm(dispatch.astype(BF16), tok, NN)
        slot_grad = mm(combine.astype(BF16), grad_ref[j], NN)
        put_image(stage_ref, slot_in, 0, i * each + j, images, slots)
        put_image(stage_ref, slot_grad, 1, i * each + j, images, slots)

    @pl.when(i == pl.num_programs(0) - 1)
    def _():
        pack_rows(stage_ref, packed_ref)


def gather_slots(tokens, out_grad, router, each):
    images, toks, width = tokens.shape
    slots = router.shape[0]
    packed = (slots, 2 * images * width // LANES, LANES)
    image = lambda i: (i, 0, 0)
    return pl.pallas_call(
        functools.partial(gather_body, images),
        grid=(images // each,),
        in_specs=[
            pl.BlockSpec((each, toks, width), image),
            pl.BlockSpec((each, toks, width), image),
            pl.BlockSpec((slots, width), lambda i: (0, 0)),
        ],
        out_specs=[
            pl.BlockSpec((each, slots, toks), image),
            pl.BlockSpec((each, slots, toks), image),
            pl.BlockSpec(packed, lambda i: (0, 0, 0)),
        ],
        out_shape=[
            jax.ShapeDtypeStruct((images, slots, toks), F32),
            jax.ShapeDtypeStruct((images, slots, toks), F32),
            jax.ShapeDtypeStruct(packed, BF16),
        ],
        scratch_shapes=[stage_shape(packed)],
        compiler_params=params(),
        name="gather_slots",
    )(tokens, out_grad, router)


def expert_body(images, packed_ref, w_in_ref, w_out_ref, act_ref, dhid_ref, back_ref,
                stage_ref, in_ref, grad_ref, out_acc, back_acc):
    f = pl.program_id(0)
    groups = packed_ref.shape[0]

    @pl.when(f == 0)
    def _():
        stage_rows((packed_ref,), stage_ref)
        load_rows(stage_ref, in_ref, 0, 0, images, groups)
        load_rows(stage_ref, grad_ref, 0, 1, images, groups)
        out_acc[...] = jnp.zeros_like(out_acc)
        back_acc[...] = jnp.zeros_like(back_acc)

    w_in, w_out = w_in_ref[0], w_out_ref[0]
    act, slope = gelu_parts(mm(in_ref[...], w_in, NN))
    act = act.astype(BF16)
    act_ref[...] = act
    dhid = (mm(grad_ref[...], w_out, NT) * slope).astype(BF16)
    dhid_ref[...] = dhid
    out_acc[...] += mm(act, w_out, NN)
    back_acc[...] += mm(dhid, w_in, NT)

    @pl.when(f == pl.num_programs(0) - 1)
    def _():
        for image in range(images):
            where = slice(image * groups, (image + 1) * groups)
            put_image(stage_ref, out_acc[where, :], 0, image, images, groups)
            put_image(stage_ref, back_acc[where, :], 1, image, images, groups)
        pack_rows(stage_ref, back_ref)


def experts(packed, w_in, w_out, block):
    width, hidden = w_in.shape[1:]
    groups = packed.shape[0]
    rows = packed.shape[1] * LANES // (2 * width) * groups
    return pl.pallas_call(
        functools.partial(expert_body, rows // groups),
        grid=(hidden // block,),
        in_specs=[
            pl.BlockSpec(packed.shape, lambda f: (0, 0, 0)),
            pl.BlockSpec((1, width, block), lambda f: (0, 0, f)),
            pl.BlockSpec((1, block, width), lambda f: (0, f, 0)),
        ],
        out_specs=[
            pl.BlockSpec((rows, block), lambda f: (0, f)),
            pl.BlockSpec((rows, block), lambda f: (0, f)),
            pl.BlockSpec(packed.shape, lambda f: (0, 0, 0)),
        ],
        out_shape=[
            jax.ShapeDtypeStruct((rows, hidden), BF16),
            jax.ShapeDtypeStruct((rows, hidden), BF16),
            jax.ShapeDtypeStruct(packed.shape, BF16),
        ],
        scratch_shapes=[
            stage_shape(packed.shape),
            pltpu.VMEM((rows, width), BF16),
            pltpu.VMEM((rows, width), BF16),
            pltpu.VMEM((rows, width), F32),
            pltpu.VMEM((rows, width), F32),
        ],
        compiler_params=params(),
        name="experts",
    )(packed, w_in, w_out)


def logit_body(images, packed_ref, tokens_ref, grad_ref, disp_ref, comb_ref, lgrad_ref, sback_ref, router_ref,
               stage_ref, acc_ref):
    i = pl.program_id(0)
    slots = packed_ref.shape[0]

    @pl.when(i == 0)
    def _():
        stage_rows((packed_ref,), stage_ref)
        acc_ref[...] = jnp.zeros_like(acc_ref)

    each = tokens_ref.shape[0]
    for j in range(each):
        slot_out = image_rows(stage_ref, 0, i * each + j, images, slots)
        slot_back = image_rows(stage_ref, 1, i * each + j, images, slots)
        sback_ref[j] = slot_back
        tok = tokens_ref[j]
        comb_dot = mm(slot_out, grad_ref[j], NT)
        disp_dot = mm(slot_back, tok, NT)
        combine, dispatch = comb_ref[j], disp_ref[j]
        comb_part = combine * (comb_dot - jnp.sum(combine * comb_dot, axis=0, keepdims=True))
        disp_part = dispatch * (disp_dot - jnp.sum(dispatch * disp_dot, axis=1, keepdims=True))
        lgrad = (comb_part + disp_part).astype(BF16)
        lgrad_ref[j] = lgrad
        acc_ref[...] += mm(lgrad, tok, NN)

    @pl.when(i == pl.num_programs(0) - 1)
    def _():
        tiles = 0
        for first in range(0, slots, SUBLANES):
            for col in range(0, acc_ref.shape[1], LANES):
                tile = acc_ref[first : first + SUBLANES, col : col + LANES]
                router_ref[tiles] = tile.astype(BF16)
                tiles += 1
        router_ref[tiles:] = jnp.zeros((router_ref.shape[0] - tiles, SUBLANES, LANES), BF16)


def logit_grads(packed, tokens, out_grad, dispatch, combine, devices, each):
    images, toks, width = tokens.shape
    slots = packed.shape[0]
    assert slots * width <= devices * SUBLANES * LANES
    image = lambda i: (i, 0, 0)
    return pl.pallas_call(
        functools.partial(logit_body, images),
        grid=(images // each,),
        in_specs=[
            pl.BlockSpec(packed.shape, lambda i: (0, 0, 0)),
            pl.BlockSpec((each, toks, width), image),
            pl.BlockSpec((each, toks, width), image),
            pl.BlockSpec((each, slots, toks), image),
            pl.BlockSpec((each, slots, toks), image),
        ],
        out_specs=[
            pl.BlockSpec((each, slots, toks), image),
            pl.BlockSpec((each, slots, width), image),
            pl.BlockSpec((devices, SUBLANES, LANES), lambda i: (0, 0, 0)),
        ],
        out_shape=[
            jax.ShapeDtypeStruct((images, slots, toks), BF16),
            jax.ShapeDtypeStruct((images, slots, width), BF16),
            jax.ShapeDtypeStruct((devices, SUBLANES, LANES), BF16),
        ],
        scratch_shapes=[
            stage_shape(packed.shape),
            pltpu.VMEM((slots, width), F32),
        ],
        compiler_params=params(),
        name="logit_grads",
    )(packed, tokens, out_grad, dispatch, combine)


def token_body(lgrad_ref, disp_ref, sback_ref, router_ref, out_ref):
    for j in range(out_ref.shape[0]):
        left = jnp.concatenate([lgrad_ref[j], disp_ref[j].astype(BF16)], axis=0)
        right = jnp.concatenate([router_ref[...], sback_ref[j]], axis=0)
        out_ref[j] = mm(left, right, TN).astype(BF16)


def token_grads(lgrad, dispatch, slot_back, router, each):
    images, slots, toks = lgrad.shape
    width = router.shape[1]
    image = lambda i: (i, 0, 0)
    return pl.pallas_call(
        token_body,
        grid=(images // each,),
        in_specs=[
            pl.BlockSpec((each, slots, toks), image),
            pl.BlockSpec((each, slots, toks), image),
            pl.BlockSpec((each, slots, width), image),
            pl.BlockSpec((slots, width), lambda i: (0, 0)),
        ],
        out_specs=pl.BlockSpec((each, toks, width), image),
        out_shape=jax.ShapeDtypeStruct((images, toks, width), BF16),
        compiler_params=params(127 * 2**19),
        name="token_grads",
    )(lgrad, dispatch, slot_back, router)


def weight_body(images, n_packed, n_own, n_first, start_ref, *refs):
    del start_ref
    packed_refs, refs = refs[:n_packed], refs[n_packed:]
    (w_in_ref, w_out_ref), refs = refs[:2], refs[2:]
    own_refs, refs = refs[:n_own], refs[n_own:]
    first_refs, refs = refs[:n_first], refs[n_first:]
    gin_ref, gout_ref, stage_ref, in_ref, grad_ref = refs[:5]
    groups = sum(packed_ref.shape[0] for packed_ref in packed_refs)

    @pl.when(pl.program_id(0) == 0)
    def _():
        stage_rows(packed_refs, stage_ref)
        load_rows(stage_ref, in_ref, 0, 0, images, groups)
        load_rows(stage_ref, grad_ref, 0, 1, images, groups)
        if n_own:
            own_stage_ref, own_in_ref, own_grad_ref = refs[5:]
            own_groups = own_refs[0].shape[0]
            stage_rows(own_refs[:1], own_stage_ref)
            load_rows(own_stage_ref, own_in_ref, 0, 0, images, own_groups)
            load_rows(own_stage_ref, own_grad_ref, 0, 1, images, own_groups)

    act, slope = gelu_parts(mm(in_ref[...], w_in_ref[0], NN))
    dhid = (mm(grad_ref[...], w_out_ref[0], NT) * slope).astype(BF16)
    gin = mm(in_ref[...], dhid, TN)
    gout = mm(act.astype(BF16), grad_ref[...], TN)
    if n_own:
        own_in_ref, own_grad_ref = refs[6:]
        _, own_act_ref, own_dhid_ref = own_refs
        gin += mm(own_in_ref[...], own_dhid_ref[...], TN)
        gout += mm(own_act_ref[...], own_grad_ref[...], TN)
    if n_first:
        gin += first_refs[0][0].astype(F32)
        gout += first_refs[1][0].astype(F32)
    gin_ref[0] = gin.astype(gin_ref.dtype)
    gout_ref[0] = gout.astype(gout_ref.dtype)


def weight_grads(start, packed, w_in, w_out, own, first, block, reps, dtype, name):
    width, hidden = w_in.shape[1], w_in.shape[2] // reps
    groups, pieces = sum(p.shape[0] for p in packed), packed[0].shape[1]
    images = pieces * LANES // (2 * width)
    rows = images * groups
    in_specs = [pl.BlockSpec(v.shape, lambda f, s: (0, 0, 0)) for v in packed]
    in_specs += [
        pl.BlockSpec((1, width, block), lambda f, s: (0, 0, s[0] + f)),
        pl.BlockSpec((1, block, width), lambda f, s: (0, s[0] + f, 0)),
    ]
    if own:
        own_rows = own[1].shape[0]
        in_specs += [pl.BlockSpec(own[0].shape, lambda f, s: (0, 0, 0))]
        in_specs += [pl.BlockSpec((own_rows, block), lambda f, s: (0, s[0] + f))] * 2
    outs = [
        pl.BlockSpec((1, width, block), lambda f, s: (0, 0, f)),
        pl.BlockSpec((1, block, width), lambda f, s: (0, f, 0)),
    ]
    if first:
        in_specs += outs
    scratch = [stage_shape((groups, pieces)), pltpu.VMEM((rows, width), BF16), pltpu.VMEM((rows, width), BF16)]
    if own:
        scratch += [stage_shape(own[0].shape)] + [pltpu.VMEM((own_rows, width), BF16)] * 2
    return pl.pallas_call(
        functools.partial(weight_body, images, len(packed), len(own), len(first)),
        grid_spec=pltpu.PrefetchScalarGridSpec(
            num_scalar_prefetch=1,
            grid=(hidden // block,),
            in_specs=in_specs,
            out_specs=outs,
            scratch_shapes=scratch,
        ),
        out_shape=[
            jax.ShapeDtypeStruct((1, width, hidden), dtype),
            jax.ShapeDtypeStruct((1, hidden, width), dtype),
        ],
        compiler_params=params(),
        name=name,
    )(start, *packed, w_in, w_out, *own, *first)


def swap(value, axis):
    return lax.all_to_all(value, axis, split_axis=0, concat_axis=0, tiled=True)


def per_device(tokens, out_grad, router, w_in, w_out):
    reps = lax.axis_size("rep")
    devices = lax.axis_size("exp") * reps
    slots, width = router.shape
    dispatch, combine, to_experts = gather_slots(tokens, out_grad, router, 3)
    own = swap(to_experts, "exp")
    act, dhid, to_images = experts(own, w_in, w_out, 512)
    hidden, block = w_in.shape[2] // reps, 640
    start = (lax.axis_index("rep") * (hidden // block)).astype(jnp.int32).reshape(1)
    pairs = [(i, i ^ 1) for i in range(reps)]
    cut = own.shape[0] * 7 // 16
    peer_first = lax.ppermute(own[:cut], "rep", pairs)
    peer_last = lax.ppermute(own[cut:], "rep", pairs)
    to_images, peer_first = lax.optimization_barrier((to_images, peer_first))
    back = swap(to_images, "exp")
    first = weight_grads(start, [peer_first], w_in, w_out, (own, act, dhid), (), block, reps, BF16, "weight_first")
    back, first = lax.optimization_barrier((back, first))
    lgrad, slot_back, tiles = logit_grads(back, tokens, out_grad, dispatch, combine, devices, 2)
    start, tiles = lax.optimization_barrier((start, tiles))
    shares = swap(tiles, ("exp", "rep")).astype(F32)
    share = jnp.sum(shares, axis=0).astype(BF16)
    token_grad = token_grads(lgrad, dispatch, slot_back, router, 3)
    share, token_grad = lax.optimization_barrier((share, token_grad))
    start, share = lax.optimization_barrier((start, share))
    tiles = swap(jnp.broadcast_to(share[None], shares.shape), ("exp", "rep"))
    tiles = tiles[: slots * width // (SUBLANES * LANES)].reshape(slots // SUBLANES, width // LANES, SUBLANES, LANES)
    router_grad = tiles.transpose(0, 2, 1, 3).reshape(slots, width).astype(F32)
    grad_in, grad_out = weight_grads(start, [peer_last], w_in, w_out, (), first, block, reps, BF16, "weight_last")
    return token_grad, grad_in, grad_out, router_grad


def solution(mesh):
    in_specs = (
        P(("exp", "rep"), None, None),
        P(("exp", "rep"), None, None),
        P(),
        P("exp", None, None),
        P("exp", None, None),
    )
    out_specs = (P(("exp", "rep"), None, None), P("exp", None, "rep"), P("exp", "rep", None), P())
    return jax.shard_map(
        per_device, mesh=mesh, in_specs=in_specs, out_specs=out_specs, check_vma=False
    )
```
